768 devices in a mesh: space: 192 (over z, y_hi, x, core), event: 4 (over y_lo).
Axes of the slice: x: 4, y: 8 (y_hi: 2, y_lo: 4; y = y_hi * 4 + y_lo), z: 12, core: 2. Of those that a mesh axis runs over, the one named last changes fastest.
Arguments:
- green: bfloat16 [8, 512, 2, 6, 24576], P(None, 'event', None, None, 'space'), may hold values from -6 to 6
- strain: bfloat16 [96, 8, 2, 6, 24576], P('event', None, None, None, 'space'), may hold values from -6 to 6
- perturb: float32 [24576], P('space'), may hold values from -6 to 6
- pairs: int32 [96, 512], P(None, 'event'), may hold values 0 or 1
Outputs:
- hessian: float32 [24576], P(('space', 'event'))
The draws below stay inside these ranges and needn't reach their ends.
All inputs are finite; a program needn't handle non-finite values. No bound on the sum of `pairs` on one device may be relied on, other than what follows from the above.
Results may differ from the reference program's by a relative error of at most 0.00096.
Values may be sent and summed in bfloat16 or wider, within the bound.
No kernel may reach another device: no remote copies, remote signals or barrier semaphores. Data moves between devices by JAX's collectives and lax.ppermute only.
A program may use at most 32 MiB of HBM per device.

```python
import math
import jax
import jax.numpy as jnp
from jax import lax

F = 8
R = 512
C = 6
NX = 24576
E = 96


def plant(drawn, rng, least, top_value):
    place = [jax.random.randint(jax.random.fold_in(rng, axis), (), 0, length) for axis, length in enumerate(drawn.shape)]
    main_axis = drawn.shape.index(max(drawn.shape))
    next_to = place[:main_axis] + [(place[main_axis] + 1) % drawn.shape[main_axis]] + place[main_axis + 1:]
    return drawn.at[tuple(place)].set(least).at[tuple(next_to)].set(top_value)


def block_scale(key, dims, cuts, smallest, high):
    loudness, own = 1.0, jax.random.fold_in(key, 6)
    for axis_at, shards_of in cuts:
        draws = jnp.exp(jax.random.uniform(jax.random.fold_in(own, axis_at), (shards_of,), jnp.float32, smallest / len(cuts), high / len(cuts)))
        loudness = loudness * jnp.repeat(draws, dims[axis_at] // shards_of).reshape([-1 if axis == axis_at else 1 for axis in range(len(dims))])
    return loudness


def gaussian(key, extent, deviation, reach, shards=(), kind=jnp.bfloat16):
    entries = jax.random.normal(key, extent, jnp.float32) * deviation
    if len(shards) > 0:
        entries = block_scale(key, extent, shards, -0.22, 0.18) * entries
    return jnp.clip(entries, min=-reach, max=reach).astype(kind)


def setup_inputs(seed: int = 0) -> dict:
    key_of = jax.random.split(jax.random.key(seed), 5)
    green = gaussian(key_of[0], (F, R, 2, C, NX), 1.0, 6.0, ((1, 4), (4, 192)))
    strain = gaussian(key_of[1], (E, F, 2, C, NX), 1.0, 6.0, ((0, 4), (4, 192)))
    perturb = gaussian(key_of[2], (NX,), 1.0, 6.0, ((0, 192),), jnp.float32)
    pairs = plant((jax.random.randint(key_of[3], (E, R), 0, 4) < 3).astype(jnp.int32), jax.random.fold_in(key_of[3], 1), 0, 1)
    return dict(green=green, strain=strain, perturb=perturb, pairs=pairs)


def one_frequency(green_f, strain_f, perturb, mask, scale_one):
    events = strain_f.shape[0]
    receivers = green_f.shape[0]
    weighted = (strain_f.astype(jnp.float32) * perturb).astype(jnp.bfloat16)
    w_real = weighted[:, 0].reshape(events, -1)
    w_imag = weighted[:, 1].reshape(events, -1)
    combo = jnp.stack([jnp.stack([w_real, -w_imag], 1), jnp.stack([w_imag, w_real], 1)], 0)
    flat_green = green_f.reshape(receivers, 2, -1).astype(jnp.float32)
    data = scale_one * jnp.einsum('rpk,qepk->qer', flat_green, combo.astype(jnp.float32))
    resid = (data * mask[None]).astype(jnp.bfloat16)
    back_in = jnp.stack([jnp.stack([resid[0], resid[1]], 1), jnp.stack([resid[1], -resid[0]], 1)], 0)
    back = jnp.einsum('qepr,rpk->qek', back_in.astype(jnp.float32), flat_green)
    flat_strain = strain_f.reshape(events, 2, -1).astype(jnp.float32)
    terms = jnp.einsum('qek,eqk->k', back, flat_strain)
    return terms.reshape(strain_f.shape[2], -1).sum(0)

def reference(green, strain, perturb, pairs):
    freqs = green.shape[0]
    cells = perturb.shape[0]
    events = strain.shape[0]
    receivers = green.shape[1]
    scale_one = 1.0 / math.sqrt(12.0 * cells)
    scale_two = 1.0 / math.sqrt(12.0 * events * freqs * receivers)
    mask = pairs.astype(jnp.float32)
    strain_by_freq = jnp.moveaxis(strain, 1, 0)

    def step(total, items):
        green_f, strain_f = items
        return (total + one_frequency(green_f, strain_f, perturb, mask, scale_one), None)
    total, unused = lax.scan(step, jnp.zeros((cells,), jnp.float32), (green, strain_by_freq))
    return scale_two * total
```

```python
import math

import jax
import jax.numpy as jnp
from jax import lax
from jax.experimental import pallas as pl
from jax.experimental.pallas import tpu as pltpu
from jax.sharding import Mesh, PartitionSpec as P

PIECES = 2
SPACE = ("z_far", "z_near", "y_hi", "x", "core")
NEAR = ("z_near", "x", "core")
FAR = ("z_far", "y_hi")
WHOLE = pl.BlockSpec(memory_space=pltpu.VMEM)


def exchange(parts, axes):
    return lax.all_to_all(parts, axes, 0, 0, tiled=True)


def spread(block, axes):
    n = lax.axis_size(axes)
    return exchange(jnp.broadcast_to(block[None], (n,) + block.shape), axes)


def wide(ref, *at):
    return jnp.concatenate([ref[at + (c,)] for c in range(ref.shape[len(at)])], 1)


def forward_kernel(own, n_event, *refs):
    pieces, (perturb_ref, green_ref, out_ref, all_ref) = refs[:-4], refs[-4:]
    per_piece = 2 * n_event - 1
    recv = out_ref.shape[-1]
    comps, cells = all_ref.shape[1], all_ref.shape[3]
    perturb = perturb_ref[...]

    for base in range(0, len(pieces), per_piece):
        piece = pieces[base:base + per_piece]
        freqs = piece[0].shape[0]
        start = base // per_piece * freqs

        def step(i, carry):
            f = start + i
            blocks = [wide(piece[0], i).astype(jnp.float32)]
            for low, high in zip(piece[1::2], piece[2::2]):
                blocks.append(wide(low, i).astype(jnp.float32) + wide(high, i).astype(jnp.float32))
            strain = jnp.concatenate(blocks, 0)
            for c in range(comps):
                all_ref[f, c] = strain[:, c * cells:(c + 1) * cells].astype(all_ref.dtype)
            weighted = (strain * perturb).astype(jnp.bfloat16)
            both = lax.dot_general(
                weighted, wide(green_ref, f), (((1,), (1,)), ((), ())), preferred_element_type=jnp.float32
            )
            rows = []
            for k in range(n_event):
                real = both[2 * own * k:2 * own * k + own]
                imag = both[2 * own * k + own:2 * own * (k + 1)]
                rows += [real[:, :recv] - imag[:, recv:], imag[:, :recv] + real[:, recv:]]
            out_ref[f] = jnp.concatenate(rows, 0).astype(out_ref.dtype)
            return carry

        lax.fori_loop(0, freqs, step, 0, unroll=2)


def backward_kernel(own, n_event, all_ref, resid_ref, green_ref, out_ref):
    freqs, comps, n_rows, cells = all_ref.shape

    def step(f, acc):
        resid = resid_ref[f].astype(jnp.float32)
        sides = []
        for k in range(n_event):
            real = resid[2 * own * k:2 * own * k + own]
            imag = resid[2 * own * k + own:2 * own * (k + 1)]
            sides += [jnp.concatenate([real, imag], 1), jnp.concatenate([imag, -real], 1)]
        sides = jnp.concatenate(sides, 0).astype(jnp.bfloat16)
        back = jnp.dot(sides, wide(green_ref, f), preferred_element_type=jnp.float32)
        for c in range(comps):
            terms = back[:, c * cells:(c + 1) * cells] * all_ref[f, c].astype(jnp.float32)
            for j in range(0, n_rows, 8):
                acc = acc + terms[j:j + 8]
        return acc

    acc = lax.fori_loop(0, freqs, step, jnp.zeros((8, cells), jnp.float32), unroll=2)
    acc = acc.sum(0, keepdims=True)
    parts, width = out_ref.shape
    for j in range(parts):
        out_ref[j:j + 1] = acc[:, j * width:(j + 1) * width]


def hop(blocks, k):
    n = lax.axis_size("event")
    ups = [lax.ppermute(up, "event", [(i, i + 1) for i in range(k - 1, n - 1)]) for up, _ in blocks]
    downs = [lax.ppermute(down, "event", [(i, i - 1) for i in range(1, n + 1 - k)]) for _, down in blocks]
    return list(zip(ups, downs))


def body(green, strain, perturb, pairs):
    freqs, recv, _, comps, cells = green.shape
    own = strain.shape[0]
    n_event = lax.axis_size("event")
    near = lax.axis_size(NEAR)
    far = lax.axis_size(FAR)
    me = lax.axis_index("event")
    events = own * n_event
    k_all = comps * cells
    n_rows = 2 * events
    tall = freqs * n_rows // near
    scale_one = 1.0 / math.sqrt(12.0 * cells * near * far)
    scale_two = 1.0 / math.sqrt(12.0 * events * freqs * recv * n_event)

    mine = strain.transpose(1, 3, 2, 0, 4).reshape(freqs, comps, 2 * own, cells)
    flat_green = green.transpose(0, 3, 2, 1, 4).reshape(freqs, comps, 2 * recv, cells)
    share = freqs // PIECES
    pieces = [mine[h * share:(h + 1) * share] for h in range(PIECES)]
    hops = [hop([(p, p) for p in pieces], 1)]
    first, flat_green = lax.optimization_barrier((hops[0][0], flat_green))
    hops[0][0] = first
    for k in range(2, n_event):
        hops.append(hop(hops[-1], k))
    blocks = []
    for h in range(PIECES):
        blocks.append(pieces[h])
        for k in range(1, n_event):
            blocks += [hops[k - 1][h][0], hops[n_event - k - 1][h][1]]
    wide_perturb = jnp.tile(perturb, comps)[None]

    order = jnp.stack(
        [lax.dynamic_slice_in_dim(pairs, ((me - k) % n_event) * own, own, 0) for k in range(n_event)], 0
    )
    mask = jnp.broadcast_to(order.astype(jnp.float32)[:, None], (n_event, 2, own, recv))
    offset = (lax.axis_index(NEAR) * tall) % n_rows
    mask = lax.dynamic_slice_in_dim(mask.reshape(n_rows, recv), offset, tall, 0)

    macs = freqs * n_rows * k_all * 2 * recv
    params = dict(
        compiler_params=pltpu.CompilerParams(vmem_limit_bytes=16 * 2**20),
        cost_estimate=pl.CostEstimate(flops=2 * macs, bytes_accessed=6_000_000, transcendentals=0),
    )
    partial, all_strain = pl.pallas_call(
        lambda *refs: forward_kernel(own, n_event, *refs),
        in_specs=[WHOLE] * (len(blocks) + 2),
        out_specs=[WHOLE] * 2,
        out_shape=[
            jax.ShapeDtypeStruct((freqs, n_rows, recv), jnp.bfloat16),
            jax.ShapeDtypeStruct((freqs, comps, n_rows, cells), jnp.bfloat16),
        ],
        name="forward",
        **params,
    )(*blocks, wide_perturb, flat_green)
    partial, mask = lax.optimization_barrier((partial, mask))

    got = exchange(partial.reshape(near, tall, recv), NEAR)
    summed = got.astype(jnp.float32).sum(0).astype(jnp.bfloat16)
    total = spread(summed, FAR).astype(jnp.float32).sum(0)
    resid = (scale_one * total * mask).astype(jnp.bfloat16)
    resid = spread(resid, NEAR).reshape(freqs, n_rows, recv)

    local_cells = pl.pallas_call(
        lambda *refs: backward_kernel(own, n_event, *refs),
        in_specs=[WHOLE] * 3,
        out_specs=WHOLE,
        out_shape=jax.ShapeDtypeStruct((n_event, cells // n_event), jnp.float32),
        name="backward",
        **params,
    )(all_strain, resid, flat_green)
    got = exchange(local_cells, "event")
    return scale_two * got.sum(0)


def solution(mesh):
    n_event = mesh.shape["event"]
    fine = Mesh(mesh.devices.reshape(6, 2, 2, 4, 2, n_event), SPACE + ("event",))
    in_specs = (
        P(None, "event", None, None, SPACE),
        P("event", None, None, None, SPACE),
        P(SPACE),
        P(None, "event"),
    )
    out_specs = P(SPACE + ("event",))
    return jax.shard_map(body, mesh=fine, in_specs=in_specs, out_specs=out_specs, check_vma=False)
```

```python
import functools
import math

import jax
import jax.numpy as jnp
from jax import lax
from jax.experimental import pallas as pl
from jax.experimental.pallas import tpu as pltpu
from jax.sharding import Mesh, PartitionSpec as P

PIECES = 2
SPACE = ("z_far", "z_near", "y_hi", "x", "core")
NEAR = ("z_near", "x", "core")
FAR = ("z_far", "y_hi")
WHOLE = pl.BlockSpec(memory_space=pltpu.VMEM)


def exchange(parts, axes):
    return lax.all_to_all(parts, axes, 0, 0, tiled=True)


def wide(ref, *at):
    return jnp.concatenate([ref[at + (c,)] for c in range(ref.shape[len(at)])], 1)


def call(kernel, name, macs, outs, *args):
    single = not isinstance(outs, list)
    return pl.pallas_call(
        kernel,
        in_specs=[WHOLE] * len(args),
        out_specs=WHOLE if single else [WHOLE] * len(outs),
        out_shape=outs,
        name=name,
        compiler_params=pltpu.CompilerParams(vmem_limit_bytes=16 * 2**20),
        cost_estimate=pl.CostEstimate(flops=2 * macs, bytes_accessed=2_000_000, transcendentals=0),
    )(*args)


def forward_kernel(own, n_event, start, *refs):
    done, piece = refs[:1 if start else 0], refs[1 if start else 0:-4]
    perturb_ref, green_ref, out_ref, all_ref = refs[-4:]
    if done:
        out_ref[:start] = done[0][...]
    recv = out_ref.shape[-1]
    freqs, comps, _, cells = all_ref.shape
    perturb = perturb_ref[...]

    def step(i, carry):
        blocks = [wide(piece[0], i).astype(jnp.float32)]
        for low, high in zip(piece[1::2], piece[2::2]):
            blocks.append(wide(low, i).astype(jnp.float32) + wide(high, i).astype(jnp.float32))
        strain = jnp.concatenate(blocks, 0)
        for c in range(comps):
            all_ref[i, c] = strain[:, c * cells:(c + 1) * cells].astype(all_ref.dtype)
        weighted = (strain * perturb).astype(jnp.bfloat16)
        both = lax.dot_general(
            weighted, wide(green_ref, start + i), (((1,), (1,)), ((), ())), preferred_element_type=jnp.float32
        )
        rows = []
        for k in range(n_event):
            real = both[2 * own * k:2 * own * k + own]
            imag = both[2 * own * k + own:2 * own * (k + 1)]
            rows += [real[:, :recv] - imag[:, recv:], imag[:, :recv] + real[:, recv:]]
        out_ref[start + i] = jnp.concatenate(rows, 0).astype(out_ref.dtype)
        return carry

    lax.fori_loop(0, freqs, step, 0, unroll=2)


def near_sum_kernel(parts_ref, out_ref):
    total = parts_ref[0].astype(jnp.float32)
    for i in range(1, parts_ref.shape[0]):
        total = total + parts_ref[i].astype(jnp.float32)
    total = total.astype(out_ref.dtype)
    for i in range(out_ref.shape[0]):
        out_ref[i] = total


def resid_kernel(scale, own, parts_ref, pairs_ref, out_ref):
    total = parts_ref[0].astype(jnp.float32)
    for i in range(1, parts_ref.shape[0]):
        total = total + parts_ref[i].astype(jnp.float32)
    mask = pairs_ref[...].astype(jnp.float32)
    mask = [mask[j:j + own] for j in range(0, mask.shape[0], own)]
    mask = jnp.concatenate([m for m in mask for _ in range(2)], 0)
    resid = (scale * total * mask).astype(out_ref.dtype)
    for i in range(out_ref.shape[0]):
        out_ref[i] = resid


def backward_kernel(own, n_event, *refs):
    pieces, (resid_ref, green_ref, out_ref) = refs[:-3], refs[-3:]
    freqs, comps, n_rows, cells = pieces[0].shape
    acc = jnp.zeros((8, cells), jnp.float32)

    for h, all_ref in enumerate(pieces):

        def step(i, acc):
            resid = resid_ref[h * freqs + i].astype(jnp.float32)
            sides = []
            for k in range(n_event):
                real = resid[2 * own * k:2 * own * k + own]
                imag = resid[2 * own * k + own:2 * own * (k + 1)]
                sides += [jnp.concatenate([real, imag], 1), jnp.concatenate([imag, -real], 1)]
            sides = jnp.concatenate(sides, 0).astype(jnp.bfloat16)
            back = jnp.dot(sides, wide(green_ref, h * freqs + i), preferred_element_type=jnp.float32)
            for c in range(comps):
                terms = back[:, c * cells:(c + 1) * cells] * all_ref[i, c].astype(jnp.float32)
                for j in range(0, n_rows, 8):
                    acc = acc + terms[j:j + 8]
            return acc

        acc = lax.fori_loop(0, freqs, step, acc, unroll=2)
    acc = acc.sum(0, keepdims=True)
    parts, width = out_ref.shape
    for j in range(parts):
        out_ref[j:j + 1] = acc[:, j * width:(j + 1) * width]


def hop(blocks, k):
    n = lax.axis_size("event")
    ups = [lax.ppermute(up, "event", [(i, i + 1) for i in range(k - 1, n - 1)]) for up, _ in blocks]
    downs = [lax.ppermute(down, "event", [(i, i - 1) for i in range(1, n + 1 - k)]) for _, down in blocks]
    return list(zip(ups, downs))


def body(green, strain, perturb, pairs):
    freqs, recv, _, comps, cells = green.shape
    own = strain.shape[0]
    n_event = lax.axis_size("event")
    near = lax.axis_size(NEAR)
    far = lax.axis_size(FAR)
    me = lax.axis_index("event")
    events = own * n_event
    n_rows = 2 * events
    share = freqs // PIECES
    tall = freqs * n_rows // near
    scale_one = 1.0 / math.sqrt(12.0 * cells * near * far)
    scale_two = 1.0 / math.sqrt(12.0 * events * freqs * recv * n_event)
    bf16 = functools.partial(jax.ShapeDtypeStruct, dtype=jnp.bfloat16)

    mine = strain.transpose(1, 3, 2, 0, 4).reshape(freqs, comps, 2 * own, cells)
    pieces = [mine[h * share:(h + 1) * share] for h in range(PIECES)]
    hops = [hop([(p, p) for p in pieces], 1)]
    for k in range(2, n_event):
        if k == n_event - 1:
            last, green = lax.optimization_barrier((hops[-1][-1], green))
            hops[-1][-1] = last
        hops.append(hop(hops[-1], k))
    flat_green = green.transpose(0, 3, 2, 1, 4).reshape(freqs, comps, 2 * recv, cells)

    wide_perturb = jnp.tile(perturb, comps)[None]
    count = tall // (2 * own)
    block = lax.axis_index(NEAR) * count % n_event
    recorded = jnp.concatenate(
        [lax.dynamic_slice_in_dim(pairs, (me - block - j) % n_event * own, own, 0) for j in range(count)], 0
    )

    macs = share * n_rows * comps * cells * 2 * recv
    done, all_strain = [], []
    for h in range(PIECES):
        blocks = [pieces[h]]
        for k in range(1, n_event):
            blocks += [hops[k - 1][h][0], hops[n_event - k - 1][h][1]]
        if h == PIECES - 1:
            blocks, done, recorded = lax.optimization_barrier((blocks, done, recorded))
        partial, part = call(
            functools.partial(forward_kernel, own, n_event, h * share),
            "forward",
            macs,
            [bf16(((h + 1) * share, n_rows, recv)), bf16((share, comps, n_rows, cells))],
            *done, *blocks, wide_perturb, flat_green,
        )
        done = [partial]
        all_strain.append(part)

    got = exchange(partial.reshape(near, tall, recv), NEAR)
    summed = exchange(call(near_sum_kernel, "near_sum", 0, bf16((far, tall, recv)), got), FAR)
    resid = call(
        functools.partial(resid_kernel, scale_one, own), "resid", 0, bf16((near, tall, recv)), summed, recorded
    )
    resid = exchange(resid, NEAR).reshape(freqs, n_rows, recv)
    local_cells = call(
        functools.partial(backward_kernel, own, n_event),
        "backward",
        PIECES * macs,
        jax.ShapeDtypeStruct((n_event, cells // n_event), jnp.float32),
        *all_strain, resid, flat_green,
    )
    return scale_two * exchange(local_cells, "event").sum(0)


def solution(mesh):
    n_event = mesh.shape["event"]
    fine = Mesh(mesh.devices.reshape(6, 2, 2, 4, 2, n_event), SPACE + ("event",))
    in_specs = (
        P(None, "event", None, None, SPACE),
        P("event", None, None, None, SPACE),
        P(SPACE),
        P(None, "event"),
    )
    out_specs = P(SPACE + ("event",))
    return jax.shard_map(body, mesh=fine, in_specs=in_specs, out_specs=out_specs, check_vma=False)
```

```python
import functools
import math

import jax
import jax.numpy as jnp
from jax import lax
from jax.experimental import pallas as pl
from jax.experimental.pallas import tpu as pltpu
from jax.sharding import Mesh, PartitionSpec as P

PIECES = 2
SPACE = ("z_far", "z_near", "y_hi", "x", "core")
NEAR = ("z_near", "x", "core")
FAR = ("z_far",)
WHOLE = pl.BlockSpec(memory_space=pltpu.VMEM)


def exchange(parts, axes):
    return lax.all_to_all(parts, axes, 0, 0, tiled=True)


def wide(ref, *at):
    return jnp.concatenate([ref[at + (c,)] for c in range(ref.shape[len(at)])], 1)


def call(kernel, name, macs, outs, *args):
    single = not isinstance(outs, list)
    return pl.pallas_call(
        kernel,
        in_specs=[WHOLE] * len(args),
        out_specs=WHOLE if single else [WHOLE] * len(outs),
        out_shape=outs,
        name=name,
        compiler_params=pltpu.CompilerParams(vmem_limit_bytes=16 * 2**20),
        cost_estimate=pl.CostEstimate(flops=2 * macs, bytes_accessed=2_000_000, transcendentals=0),
    )(*args)


def forward_kernel(own, n_event, start, *refs):
    done, piece = refs[:1 if start else 0], refs[1 if start else 0:-4]
    perturb_ref, green_ref, out_ref, all_ref = refs[-4:]
    if done:
        out_ref[:start] = done[0][...]
    recv = out_ref.shape[-1]
    freqs, comps, _, cells = all_ref.shape
    perturb = perturb_ref[...]

    def step(i, carry):
        blocks = [wide(piece[0], i).astype(jnp.float32)]
        for low, high in zip(piece[1::2], piece[2::2]):
            blocks.append(wide(low, i).astype(jnp.float32) + wide(high, i).astype(jnp.float32))
        strain = jnp.concatenate(blocks, 0)
        for c in range(comps):
            all_ref[i, c] = strain[:, c * cells:(c + 1) * cells].astype(all_ref.dtype)
        weighted = (strain * perturb).astype(jnp.bfloat16)
        both = lax.dot_general(
            weighted, wide(green_ref, start + i), (((1,), (1,)), ((), ())), preferred_element_type=jnp.float32
        )
        rows = []
        for k in range(n_event):
            real = both[2 * own * k:2 * own * k + own]
            imag = both[2 * own * k + own:2 * own * (k + 1)]
            rows += [real[:, :recv] - imag[:, recv:], imag[:, :recv] + real[:, recv:]]
        out_ref[start + i] = jnp.concatenate(rows, 0).astype(out_ref.dtype)
        return carry

    lax.fori_loop(0, freqs, step, 0, unroll=2)


def near_sum_kernel(parts_ref, out_ref):
    total = parts_ref[0].astype(jnp.float32)
    for i in range(1, parts_ref.shape[0]):
        total = total + parts_ref[i].astype(jnp.float32)
    total = total.astype(out_ref.dtype)
    for i in range(out_ref.shape[0]):
        out_ref[i] = total


def far_sum_kernel(parts_ref, out_ref):
    total = parts_ref[0].astype(jnp.float32)
    for i in range(1, parts_ref.shape[0]):
        total = total + parts_ref[i].astype(jnp.float32)
    out_ref[...] = total


def resid_kernel(scale, own, mine_ref, other_ref, pairs_ref, out_ref):
    total = mine_ref[...] + other_ref[...]
    mask = pairs_ref[...].astype(jnp.float32)
    mask = [mask[j:j + own] for j in range(0, mask.shape[0], own)]
    mask = jnp.concatenate([m for m in mask for _ in range(2)], 0)
    resid = (scale * total * mask).astype(out_ref.dtype)
    for i in range(out_ref.shape[0]):
        out_ref[i] = resid


def backward_kernel(own, n_event, *refs):
    pieces, (resid_ref, green_ref, out_ref) = refs[:-3], refs[-3:]
    freqs, comps, n_rows, cells = pieces[0].shape
    acc = jnp.zeros((8, cells), jnp.float32)

    for h, all_ref in enumerate(pieces):

        def step(i, acc):
            resid = resid_ref[h * freqs + i].astype(jnp.float32)
            sides = []
            for k in range(n_event):
                real = resid[2 * own * k:2 * own * k + own]
                imag = resid[2 * own * k + own:2 * own * (k + 1)]
                sides += [jnp.concatenate([real, imag], 1), jnp.concatenate([imag, -real], 1)]
            sides = jnp.concatenate(sides, 0).astype(jnp.bfloat16)
            back = jnp.dot(sides, wide(green_ref, h * freqs + i), preferred_element_type=jnp.float32)
            for c in range(comps):
                terms = back[:, c * cells:(c + 1) * cells] * all_ref[i, c].astype(jnp.float32)
                for j in range(0, n_rows, 8):
                    acc = acc + terms[j:j + 8]
            return acc

        acc = lax.fori_loop(0, freqs, step, acc, unroll=2)
    acc = acc.sum(0, keepdims=True)
    parts, width = out_ref.shape
    for j in range(parts):
        out_ref[j:j + 1] = acc[:, j * width:(j + 1) * width]


def hop(blocks, k):
    n = lax.axis_size("event")
    ups = [lax.ppermute(up, "event", [(i, i + 1) for i in range(k - 1, n - 1)]) for up, _ in blocks]
    downs = [lax.ppermute(down, "event", [(i, i - 1) for i in range(1, n + 1 - k)]) for _, down in blocks]
    return list(zip(ups, downs))


def body(green, strain, perturb, pairs):
    freqs, recv, _, comps, cells = green.shape
    own = strain.shape[0]
    n_event = lax.axis_size("event")
    near = lax.axis_size(NEAR)
    far = lax.axis_size(FAR)
    me = lax.axis_index("event")
    events = own * n_event
    n_rows = 2 * events
    share = freqs // PIECES
    tall = freqs * n_rows // near
    scale_one = 1.0 / math.sqrt(12.0 * cells * near * far * lax.axis_size("y_hi"))
    scale_two = 1.0 / math.sqrt(12.0 * events * freqs * recv * n_event)
    bf16 = functools.partial(jax.ShapeDtypeStruct, dtype=jnp.bfloat16)

    pieces = []
    for h in range(PIECES):
        if h > 0:
            pieces[-1], strain = lax.optimization_barrier((pieces[-1], strain))
        part = strain[:, h * share:(h + 1) * share]
        pieces.append(part.transpose(1, 3, 2, 0, 4).reshape(share, comps, 2 * own, cells))
    hops = [hop([(p, p) for p in pieces], 1)]
    for k in range(2, n_event):
        if k == n_event - 1:
            early, green = lax.optimization_barrier((hops[-1][0], green))
            hops[-1][0] = early
        hops.append(hop(hops[-1], k))
    flat_green = green.transpose(0, 3, 2, 1, 4).reshape(freqs, comps, 2 * recv, cells)

    wide_perturb = jnp.tile(perturb, comps)[None]
    count = tall // (2 * own)
    block = lax.axis_index(NEAR) * count % n_event
    recorded = jnp.concatenate(
        [lax.dynamic_slice_in_dim(pairs, (me - block - j) % n_event * own, own, 0) for j in range(count)], 0
    )

    macs = share * n_rows * comps * cells * 2 * recv
    done, all_strain = [], []
    for h in range(PIECES):
        blocks = [pieces[h]]
        for k in range(1, n_event):
            blocks += [hops[k - 1][h][0], hops[n_event - k - 1][h][1]]
        if h == PIECES - 1:
            blocks, done, recorded = lax.optimization_barrier((blocks, done, recorded))
        partial, part = call(
            functools.partial(forward_kernel, own, n_event, h * share),
            "forward",
            macs,
            [bf16(((h + 1) * share, n_rows, recv)), bf16((share, comps, n_rows, cells))],
            *done, *blocks, wide_perturb, flat_green,
        )
        done = [partial]
        all_strain.append(part)

    got = exchange(partial.reshape(near, tall, recv), NEAR)
    summed = exchange(call(near_sum_kernel, "near_sum", 0, bf16((far, tall, recv)), got), FAR)
    summed = call(far_sum_kernel, "far_sum", 0, jax.ShapeDtypeStruct((tall, recv), jnp.float32), summed)
    other = lax.ppermute(summed, "y_hi", [(0, 1), (1, 0)])
    resid = call(
        functools.partial(resid_kernel, scale_one, own), "resid", 0, bf16((near, tall, recv)), summed, other, recorded
    )
    resid = exchange(resid, NEAR).reshape(freqs, n_rows, recv)
    local_cells = call(
        functools.partial(backward_kernel, own, n_event),
        "backward",
        PIECES * macs,
        jax.ShapeDtypeStruct((n_event, cells // n_event), jnp.float32),
        *all_strain, resid, flat_green,
    )
    return scale_two * exchange(local_cells, "event").sum(0)


def solution(mesh):
    n_event = mesh.shape["event"]
    fine = Mesh(mesh.devices.reshape(6, 2, 2, 4, 2, n_event), SPACE + ("event",))
    in_specs = (
        P(None, "event", None, None, SPACE),
        P("event", None, None, None, SPACE),
        P(SPACE),
        P(None, "event"),
    )
    out_specs = P(SPACE + ("event",))
    return jax.shard_map(body, mesh=fine, in_specs=in_specs, out_specs=out_specs, check_vma=False)
```

```python
import functools
import math

import jax
import jax.numpy as jnp
from jax import lax
from jax.experimental import pallas as pl
from jax.experimental.pallas import tpu as pltpu
from jax.sharding import Mesh, PartitionSpec as P

PIECES = 2
SPACE = ("z_far", "z_near", "y_hi", "x", "core")
NEAR = ("z_near", "x", "core")
FAR = ("z_far",)
WHOLE = pl.BlockSpec(memory_space=pltpu.VMEM)


def exchange(parts, axes):
    return lax.all_to_all(parts, axes, 0, 0, tiled=True)


def wide(ref, *at):
    return jnp.concatenate([ref[at + (c,)] for c in range(ref.shape[len(at)])], 1)


def call(kernel, name, macs, outs, *args):
    single = not isinstance(outs, list)
    return pl.pallas_call(
        kernel,
        in_specs=[WHOLE] * len(args),
        out_specs=WHOLE if single else [WHOLE] * len(outs),
        out_shape=outs,
        name=name,
        compiler_params=pltpu.CompilerParams(vmem_limit_bytes=16 * 2**20),
        cost_estimate=pl.CostEstimate(flops=2 * macs, bytes_accessed=2_000_000, transcendentals=0),
    )(*args)


def forward_kernel(own, n_event, start, *refs):
    done, piece = refs[:1 if start else 0], refs[1 if start else 0:-4]
    perturb_ref, green_ref, out_ref, all_ref = refs[-4:]
    if done:
        out_ref[:start] = done[0][...]
    recv = out_ref.shape[-1]
    freqs, comps, _, cells = all_ref.shape
    perturb = perturb_ref[...]

    def step(i, carry):
        blocks = [wide(piece[0], i).astype(jnp.float32)]
        for low, high in zip(piece[1::2], piece[2::2]):
            blocks.append(wide(low, i).astype(jnp.float32) + wide(high, i).astype(jnp.float32))
        strain = jnp.concatenate(blocks, 0)
        for c in range(comps):
            all_ref[i, c] = strain[:, c * cells:(c + 1) * cells].astype(all_ref.dtype)
        weighted = (strain * perturb).astype(jnp.bfloat16)
        both = lax.dot_general(
            weighted, wide(green_ref, start + i), (((1,), (1,)), ((), ())), preferred_element_type=jnp.float32
        )
        rows = []
        for k in range(n_event):
            real = both[2 * own * k:2 * own * k + own]
            imag = both[2 * own * k + own:2 * own * (k + 1)]
            rows += [real[:, :recv] - imag[:, recv:], imag[:, :recv] + real[:, recv:]]
        out_ref[start + i] = jnp.concatenate(rows, 0).astype(out_ref.dtype)
        return carry

    lax.fori_loop(0, freqs, step, 0, unroll=2)


def near_sum_kernel(parts_ref, out_ref):
    total = parts_ref[0].astype(jnp.float32)
    for i in range(1, parts_ref.shape[0]):
        total = total + parts_ref[i].astype(jnp.float32)
    total = total.astype(out_ref.dtype)
    for i in range(out_ref.shape[0]):
        out_ref[i] = total


def far_sum_kernel(parts_ref, out_ref, send_ref):
    total = parts_ref[0].astype(jnp.float32)
    for i in range(1, parts_ref.shape[0]):
        total = total + parts_ref[i].astype(jnp.float32)
    out_ref[...] = total
    send_ref[...] = total.astype(send_ref.dtype)


def resid_kernel(scale, own, mine_ref, other_ref, pairs_ref, out_ref):
    total = mine_ref[...] + other_ref[...].astype(jnp.float32)
    mask = pairs_ref[...].astype(jnp.float32)
    mask = [mask[j:j + own] for j in range(0, mask.shape[0], own)]
    mask = jnp.concatenate([m for m in mask for _ in range(2)], 0)
    resid = (scale * total * mask).astype(out_ref.dtype)
    for i in range(out_ref.shape[0]):
        out_ref[i] = resid


def backward_kernel(own, n_event, *refs):
    pieces, (resid_ref, green_ref, out_ref) = refs[:-3], refs[-3:]
    freqs, comps, n_rows, cells = pieces[0].shape
    acc = jnp.zeros((8, cells), jnp.float32)

    for h, all_ref in enumerate(pieces):

        def step(i, acc):
            resid = resid_ref[h * freqs + i].astype(jnp.float32)
            sides = []
            for k in range(n_event):
                real = resid[2 * own * k:2 * own * k + own]
                imag = resid[2 * own * k + own:2 * own * (k + 1)]
                sides += [jnp.concatenate([real, imag], 1), jnp.concatenate([imag, -real], 1)]
            sides = jnp.concatenate(sides, 0).astype(jnp.bfloat16)
            back = jnp.dot(sides, wide(green_ref, h * freqs + i), preferred_element_type=jnp.float32)
            for c in range(comps):
                terms = back[:, c * cells:(c + 1) * cells] * all_ref[i, c].astype(jnp.float32)
                for j in range(0, n_rows, 8):
                    acc = acc + terms[j:j + 8]
            return acc

        acc = lax.fori_loop(0, freqs, step, acc, unroll=2)
    acc = acc.sum(0, keepdims=True)
    parts, width = out_ref.shape
    for j in range(parts):
        out_ref[j:j + 1] = acc[:, j * width:(j + 1) * width]


def hop(blocks, k):
    n = lax.axis_size("event")
    ups = [lax.ppermute(up, "event", [(i, i + 1) for i in range(k - 1, n - 1)]) for up, _ in blocks]
    downs = [lax.ppermute(down, "event", [(i, i - 1) for i in range(1, n + 1 - k)]) for _, down in blocks]
    return list(zip(ups, downs))


def body(green, strain, perturb, pairs):
    freqs, recv, _, comps, cells = green.shape
    own = strain.shape[0]
    n_event = lax.axis_size("event")
    near = lax.axis_size(NEAR)
    far = lax.axis_size(FAR)
    me = lax.axis_index("event")
    events = own * n_event
    n_rows = 2 * events
    share = freqs // PIECES
    tall = freqs * n_rows // near
    scale_one = 1.0 / math.sqrt(12.0 * cells * near * far * lax.axis_size("y_hi"))
    scale_two = 1.0 / math.sqrt(12.0 * events * freqs * recv * n_event)
    bf16 = functools.partial(jax.ShapeDtypeStruct, dtype=jnp.bfloat16)

    pieces = []
    for h in range(PIECES):
        if h > 0:
            pieces[-1], strain = lax.optimization_barrier((pieces[-1], strain))
        part = strain[:, h * share:(h + 1) * share]
        pieces.append(part.transpose(1, 3, 2, 0, 4).reshape(share, comps, 2 * own, cells))
    hops = [hop([(p, p) for p in pieces], 1)]
    for k in range(2, n_event):
        if k == n_event - 1:
            early, green = lax.optimization_barrier((hops[-1][0], green))
            hops[-1][0] = early
        hops.append(hop(hops[-1], k))
    flat_green = green.transpose(0, 3, 2, 1, 4).reshape(freqs, comps, 2 * recv, cells)

    wide_perturb = jnp.tile(perturb, comps)[None]
    count = tall // (2 * own)
    block = lax.axis_index(NEAR) * count % n_event
    recorded = jnp.concatenate(
        [lax.dynamic_slice_in_dim(pairs, (me - block - j) % n_event * own, own, 0) for j in range(count)], 0
    )

    macs = share * n_rows * comps * cells * 2 * recv
    done, all_strain = [], []
    for h in range(PIECES):
        blocks = [pieces[h]]
        for k in range(1, n_event):
            blocks += [hops[k - 1][h][0], hops[n_event - k - 1][h][1]]
        if h == PIECES - 1:
            blocks, done, recorded = lax.optimization_barrier((blocks, done, recorded))
        partial, part = call(
            functools.partial(forward_kernel, own, n_event, h * share),
            "forward",
            macs,
            [bf16(((h + 1) * share, n_rows, recv)), bf16((share, comps, n_rows, cells))],
            *done, *blocks, wide_perturb, flat_green,
        )
        done = [partial]
        all_strain.append(part)

    got = exchange(partial.reshape(near, tall, recv), NEAR)
    summed = exchange(call(near_sum_kernel, "near_sum", 0, bf16((far, tall, recv)), got), FAR)
    outs = [jax.ShapeDtypeStruct((tall, recv), jnp.float32), bf16((tall, recv))]
    summed, sent = call(far_sum_kernel, "far_sum", 0, outs, summed)
    other = lax.ppermute(sent, "y_hi", [(0, 1), (1, 0)])
    resid = call(
        functools.partial(resid_kernel, scale_one, own), "resid", 0, bf16((near, tall, recv)), summed, other, recorded
    )
    resid = exchange(resid, NEAR).reshape(freqs, n_rows, recv)
    local_cells = call(
        functools.partial(backward_kernel, own, n_event),
        "backward",
        PIECES * macs,
        jax.ShapeDtypeStruct((n_event, cells // n_event), jnp.float32),
        *all_strain, resid, flat_green,
    )
    return scale_two * exchange(local_cells, "event").sum(0)


def solution(mesh):
    n_event = mesh.shape["event"]
    fine = Mesh(mesh.devices.reshape(6, 2, 2, 4, 2, n_event), SPACE + ("event",))
    in_specs = (
        P(None, "event", None, None, SPACE),
        P("event", None, None, None, SPACE),
        P(SPACE),
        P(None, "event"),
    )
    out_specs = P(SPACE + ("event",))
    return jax.shard_map(body, mesh=fine, in_specs=in_specs, out_specs=out_specs, check_vma=False)
```

```python
import functools
import math

import jax
import jax.numpy as jnp
from jax import lax
from jax.experimental import pallas as pl
from jax.experimental.pallas import tpu as pltpu
from jax.sharding import Mesh, PartitionSpec as P

PIECES = 2
SPACE = ("z_far", "z_near", "y_hi", "x", "core")
NEAR = ("z_near", "x", "core")
FAR = ("z_far",)
WHOLE = pl.BlockSpec(memory_space=pltpu.VMEM)


def exchange(parts, axes):
    return lax.all_to_all(parts, axes, 0, 0, tiled=True)


def wide(ref, *at):
    return jnp.concatenate([ref[at + (c,)] for c in range(ref.shape[len(at)])], 1)


def call(kernel, name, macs, outs, *args):
    single = not isinstance(outs, list)
    return pl.pallas_call(
        kernel,
        in_specs=[WHOLE] * len(args),
        out_specs=WHOLE if single else [WHOLE] * len(outs),
        out_shape=outs,
        name=name,
        compiler_params=pltpu.CompilerParams(vmem_limit_bytes=16 * 2**20),
        cost_estimate=pl.CostEstimate(flops=2 * macs, bytes_accessed=2_000_000, transcendentals=0),
    )(*args)


def forward_kernel(own, n_event, start, *refs):
    done, piece = refs[:1 if start else 0], refs[1 if start else 0:-4]
    perturb_ref, green_ref, out_ref, all_ref = refs[-4:]
    if done:
        out_ref[:start] = done[0][...]
    recv = out_ref.shape[-1]
    freqs, comps, _, cells = all_ref.shape
    perturb = perturb_ref[...]

    def step(i, carry):
        blocks = [wide(piece[0], i).astype(jnp.float32)]
        for low, high in zip(piece[1::2], piece[2::2]):
            blocks.append(wide(low, i).astype(jnp.float32) + wide(high, i).astype(jnp.float32))
        strain = jnp.concatenate(blocks, 0)
        for c in range(comps):
            all_ref[i, c] = strain[:, c * cells:(c + 1) * cells].astype(all_ref.dtype)
        weighted = (strain * perturb).astype(jnp.bfloat16)
        both = lax.dot_general(
            weighted, wide(green_ref, start + i), (((1,), (1,)), ((), ())), preferred_element_type=jnp.float32
        )
        rows = []
        for k in range(n_event):
            real = both[2 * own * k:2 * own * k + own]
            imag = both[2 * own * k + own:2 * own * (k + 1)]
            rows += [real[:, :recv] - imag[:, recv:], imag[:, :recv] + real[:, recv:]]
        out_ref[start + i] = jnp.concatenate(rows, 0).astype(out_ref.dtype)
        return carry

    lax.fori_loop(0, freqs, step, 0, unroll=4)


def near_sum_kernel(parts_ref, out_ref):
    total = parts_ref[0].astype(jnp.float32)
    for i in range(1, parts_ref.shape[0]):
        total = total + parts_ref[i].astype(jnp.float32)
    total = total.astype(out_ref.dtype)
    for i in range(out_ref.shape[0]):
        out_ref[i] = total


def far_sum_kernel(parts_ref, out_ref):
    total = parts_ref[0].astype(jnp.float32)
    for i in range(1, parts_ref.shape[0]):
        total = total + parts_ref[i].astype(jnp.float32)
    out_ref[...] = total


def resid_kernel(scale, own, mine_ref, other_ref, pairs_ref, out_ref):
    total = mine_ref[...] + other_ref[...]
    mask = pairs_ref[...].astype(jnp.float32)
    mask = [mask[j:j + own] for j in range(0, mask.shape[0], own)]
    mask = jnp.concatenate([m for m in mask for _ in range(2)], 0)
    resid = (scale * total * mask).astype(out_ref.dtype)
    for i in range(out_ref.shape[0]):
        out_ref[i] = resid


def backward_kernel(own, n_event, *refs):
    pieces, (resid_ref, green_ref, out_ref) = refs[:-3], refs[-3:]
    freqs, comps, n_rows, cells = pieces[0].shape
    acc = jnp.zeros((8, cells), jnp.float32)

    for h, all_ref in enumerate(pieces):

        def step(i, acc):
            resid = resid_ref[h * freqs + i].astype(jnp.float32)
            sides = []
            for k in range(n_event):
                real = resid[2 * own * k:2 * own * k + own]
                imag = resid[2 * own * k + own:2 * own * (k + 1)]
                sides += [jnp.concatenate([real, imag], 1), jnp.concatenate([imag, -real], 1)]
            sides = jnp.concatenate(sides, 0).astype(jnp.bfloat16)
            back = jnp.dot(sides, wide(green_ref, h * freqs + i), preferred_element_type=jnp.float32)
            for c in range(comps):
                terms = back[:, c * cells:(c + 1) * cells] * all_ref[i, c].astype(jnp.float32)
                for j in range(0, n_rows, 8):
                    acc = acc + terms[j:j + 8]
            return acc

        acc = lax.fori_loop(0, freqs, step, acc, unroll=4)
    acc = acc.sum(0, keepdims=True)
    parts, width = out_ref.shape
    for j in range(parts):
        out_ref[j:j + 1] = acc[:, j * width:(j + 1) * width]


def hop(blocks, k):
    n = lax.axis_size("event")
    ups = [lax.ppermute(up, "event", [(i, i + 1) for i in range(k - 1, n - 1)]) for up, _ in blocks]
    downs = [lax.ppermute(down, "event", [(i, i - 1) for i in range(1, n + 1 - k)]) for _, down in blocks]
    return list(zip(ups, downs))


def body(green, strain, perturb, pairs):
    freqs, recv, _, comps, cells = green.shape
    own = strain.shape[0]
    n_event = lax.axis_size("event")
    near = lax.axis_size(NEAR)
    far = lax.axis_size(FAR)
    me = lax.axis_index("event")
    events = own * n_event
    n_rows = 2 * events
    share = freqs // PIECES
    tall = freqs * n_rows // near
    scale_one = 1.0 / math.sqrt(12.0 * cells * near * far * lax.axis_size("y_hi"))
    scale_two = 1.0 / math.sqrt(12.0 * events * freqs * recv * n_event)
    bf16 = functools.partial(jax.ShapeDtypeStruct, dtype=jnp.bfloat16)

    pieces = []
    for h in range(PIECES):
        if h > 0:
            pieces[-1], strain = lax.optimization_barrier((pieces[-1], strain))
        part = strain[:, h * share:(h + 1) * share]
        pieces.append(part.transpose(1, 3, 2, 0, 4).reshape(share, comps, 2 * own, cells))
    hops = [hop([(p, p) for p in pieces], 1)]
    for k in range(2, n_event):
        if k == n_event - 1:
            early, green = lax.optimization_barrier((hops[-1][0], green))
            hops[-1][0] = early
        hops.append(hop(hops[-1], k))
    flat_green = green.transpose(0, 3, 2, 1, 4).reshape(freqs, comps, 2 * recv, cells)

    wide_perturb = jnp.tile(perturb, comps)[None]
    count = tall // (2 * own)
    block = lax.axis_index(NEAR) * count % n_event
    recorded = jnp.concatenate(
        [lax.dynamic_slice_in_dim(pairs, (me - block - j) % n_event * own, own, 0) for j in range(count)], 0
    )

    macs = share * n_rows * comps * cells * 2 * recv
    done, all_strain = [], []
    for h in range(PIECES):
        blocks = [pieces[h]]
        for k in range(1, n_event):
            blocks += [hops[k - 1][h][0], hops[n_event - k - 1][h][1]]
        if h == PIECES - 1:
            blocks, done, recorded = lax.optimization_barrier((blocks, done, recorded))
        partial, part = call(
            functools.partial(forward_kernel, own, n_event, h * share),
            "forward",
            macs,
            [bf16(((h + 1) * share, n_rows, recv)), bf16((share, comps, n_rows, cells))],
            *done, *blocks, wide_perturb, flat_green,
        )
        done = [partial]
        all_strain.append(part)

    got = exchange(partial.reshape(near, tall, recv), NEAR)
    summed = exchange(call(near_sum_kernel, "near_sum", 0, bf16((far, tall, recv)), got), FAR)
    summed = call(far_sum_kernel, "far_sum", 0, jax.ShapeDtypeStruct((tall, recv), jnp.float32), summed)
    other = lax.ppermute(summed, "y_hi", [(0, 1), (1, 0)])
    resid = call(
        functools.partial(resid_kernel, scale_one, own), "resid", 0, bf16((near, tall, recv)), summed, other, recorded
    )
    resid = exchange(resid, NEAR).reshape(freqs, n_rows, recv)
    local_cells = call(
        functools.partial(backward_kernel, own, n_event),
        "backward",
        PIECES * macs,
        jax.ShapeDtypeStruct((n_event, cells // n_event), jnp.float32),
        *all_strain, resid, flat_green,
    )
    return scale_two * exchange(local_cells, "event").sum(0)


def solution(mesh):
    n_event = mesh.shape["event"]
    fine = Mesh(mesh.devices.reshape(6, 2, 2, 4, 2, n_event), SPACE + ("event",))
    in_specs = (
        P(None, "event", None, None, SPACE),
        P("event", None, None, None, SPACE),
        P(SPACE),
        P(None, "event"),
    )
    out_specs = P(SPACE + ("event",))
    return jax.shard_map(body, mesh=fine, in_specs=in_specs, out_specs=out_specs, check_vma=False)
```
